512 devices in a mesh: section: 8 (over x, core), expert: 64 (over z, y).
Axes of the slice: x: 4, y: 8, z: 8, core: 2. Of those that a mesh axis runs over, the one named last changes fastest.
Arguments:
- micro_inputs: bfloat16 [15, 256, 3584], P(None, 'expert'), may hold values from -6 to 6
- norm_gain: bfloat16 [8, 3584], P('section'), may hold values from 0.25 to 1.75
- gate_up: bfloat16 [8, 64, 3584, 256], P('section', 'expert'), may hold values from -0.09375 to 0.09375
- down_proj: bfloat16 [8, 64, 128, 3584], P('section', 'expert'), may hold values from -0.1875 to 0.1875
- routes: int32 [8, 8, 256, 2], P('section', None, 'expert'), may hold values from 0 to 7, all different within a row; in each aligned block of 4 rows (0 to 3, 4 to 7, ..., all dimensions but the last counted through in order) at most 2 rows name the same one
- route_weights: float32 [8, 8, 256, 2], P('section', None, 'expert'), may hold values from 0.25 to 1
Outputs:
- layer_outputs: bfloat16 [8, 8, 256, 3584], P('section', None, 'expert')
The draws below stay inside these ranges and needn't reach their ends.
Inputs may be any that keep to these rules, and one draw needn't show every extreme that they name: `routes`: in each layer and tick, among the rows of one device no expert is picked by more than 2 rows, a bound that some block reaches; each row picks 2 distinct experts.
All inputs are finite; a program needn't handle non-finite values.
Results may differ from the reference program's by a relative error of at most 0.029.
Values may be sent and summed in bfloat16 or wider, within the bound.
A program may use at most 64 MiB of HBM per device.

```python
import math
import jax
import jax.numpy as jnp
import numpy as np
from jax import lax

D = 3584
FF_DEV = 128
SHARDS = 8
FF = 1024
TOP = 2
ROWS = 4
LAYERS = 8
TICKS = 8
MICRO = 15
EXPERTS = 8
ROWS_ALL = 256
CAP = 2
N_EXPERT = 64


def shard_levels(key, shape, pieces, smallest, largest):
    level = 1.0
    for dim, shards_of in pieces:
        draws = jax.random.uniform(jax.random.fold_in(jax.random.fold_in(key, 6), dim), (shards_of,), jnp.float32, smallest / len(pieces), largest / len(pieces))
        level = level * jnp.repeat(jnp.exp(draws), shape[dim] // shards_of).reshape((-1,) + (1,) * (len(shape) - 1 - dim))
    return level


def deal_out(own_key, own, number, rows, number_of, top, reach, lean):
    ranking = jax.random.permutation(own_key, number_of)
    packed, common = shares(number_of, rows * top, reach, lean, True), shares(number_of, rows * top, reach, lean, False)
    places = jnp.arange(number_of)

    def named(tallies, offset_by):
        used = int((tallies > 0).sum())
        fixed = max(1, used // 4)
        moved = fixed + (places - fixed + offset_by * (used - fixed)) % max(1, number_of - fixed)
        return jnp.zeros((number_of,), jnp.int32).at[ranking[jnp.where(places < fixed, places, moved)]].set(jnp.asarray(tallies, jnp.int32))

    tallies = jnp.where(number % 4 == 0, named(packed, number // 4), named(common, number - number // 4 - 1))
    mixed = jax.random.permutation(jax.random.fold_in(own, 3), number_of)
    donor, taker = mixed[0:number_of // 2 * 2:2], mixed[1:number_of // 2 * 2:2]
    room = jnp.minimum(tallies[donor] - 1, reach - tallies[taker]) // 2
    room = jnp.where((donor == ranking[0]) | (taker == ranking[0]) | (tallies[taker] == 0), 0, jnp.maximum(room, 0))
    moved = jax.random.randint(jax.random.fold_in(own, 4), (number_of // 2,), 0, 1 << 20) % (room + 1)
    tallies = tallies.at[donor].add(-moved).at[taker].add(moved)
    labels = jnp.searchsorted(jnp.cumsum(tallies), jnp.arange(rows * top), side="right").astype(jnp.int32)
    listing = labels.reshape(top, rows).T
    listing = listing[jax.random.permutation(jax.random.fold_in(own, 1), rows)]
    offset_by = jax.random.randint(jax.random.fold_in(own, 2), (rows, 1), 0, top)
    return jnp.take_along_axis(listing, (jnp.arange(top)[None, :] + offset_by) % top, axis=1)


def shares(number_of, total, most, slope, full):
    weights = [(1 << 20) // math.isqrt(standing ** slope) + 1 for standing in range(1, number_of + 1)]
    largest = most if full else min(most, max(-(-total // number_of), total * weights[0] // sum(weights)))
    least = 1 if total - largest >= number_of - 1 else 0
    holding, surplus = [largest] + [least] * (number_of - 1), total - largest - least * (number_of - 1)
    while surplus > 0:
        movable = [i for i in range(1, number_of) if holding[i] < largest] or [i for i in range(1, number_of) if holding[i] < most]
        whole, remaining = sum([weights[i] for i in movable]), surplus
        for i in movable:
            addition = min(most - holding[i], max(1, remaining * weights[i] // whole), surplus)
            holding[i] = holding[i] + addition
            surplus = surplus - addition
    return np.array(holding)


def normal_values(key, extent, width, bound, split=(), held_as=jnp.bfloat16):
    result = width * jax.random.normal(key, extent, jnp.float32)
    if split:
        result = result * shard_levels(key, extent, split, -0.22, 0.18)
    return jnp.clip(result, -bound, bound).astype(held_as)


def setup_inputs(seed: int = 0) -> dict:
    arg_keys = jax.random.split(jax.random.key(seed), 7)
    micro_inputs = normal_values(arg_keys[0], (MICRO, ROWS_ALL, D), 1.0, 6.0, ((1, 64),))
    norm_gain = jnp.clip(1.0 + 0.15 * jax.random.normal(arg_keys[1], (LAYERS, D), jnp.float32), 0.25, 1.75).astype(jnp.bfloat16)
    gate_up = normal_values(arg_keys[2], (LAYERS, N_EXPERT, D, 2 * FF_DEV), D ** -0.5, 0.09375, ((0, 8), (1, 64)))
    down_proj = normal_values(arg_keys[3], (LAYERS, N_EXPERT, FF_DEV, D), FF ** -0.5, 0.1875, ((0, 8), (1, 64)))
    routes_keys = jax.random.split(jax.random.fold_in(arg_keys[4], 1), LAYERS * TICKS * ROWS_ALL // ROWS)
    routes_turns = jax.random.permutation(jax.random.fold_in(arg_keys[4], 3), LAYERS * TICKS * ROWS_ALL // ROWS)
    routes = jax.vmap(lambda own, number: deal_out(jax.random.fold_in(arg_keys[4], 2), own, number, ROWS, EXPERTS, TOP, CAP, 2))(routes_keys, routes_turns).reshape((LAYERS, TICKS, ROWS_ALL, TOP))
    route_weights = jnp.clip(jnp.exp(math.log(1.0) - 1.3862944 * jax.random.uniform(arg_keys[5], (LAYERS, TICKS, ROWS_ALL, TOP), jnp.float32) ** shard_levels(arg_keys[5], (LAYERS, TICKS, ROWS_ALL, TOP), ((0, 8), (2, 64)), -0.2, 0.2)), 0.25, 1.0)
    return {"micro_inputs": micro_inputs, "norm_gain": norm_gain, "gate_up": gate_up, "down_proj": down_proj, "routes": routes, "route_weights": route_weights}


EPSILON = 1e-06

def rounded_back(values):
    return lax.optimization_barrier(values.astype(jnp.bfloat16)).astype(jnp.float32)

def rms_normed(row_block, gain_row):
    values = row_block.astype(jnp.float32)
    scaled = values * lax.rsqrt(lax.optimization_barrier(jnp.mean(values * values, axis=1, keepdims=True)) + EPSILON)
    return (scaled * gain_row.astype(jnp.float32)).astype(jnp.bfloat16)

def moe_layer(entering, gain_row, gate_slices, down_slices, picked, picked_weights):
    values = entering.astype(jnp.float32)
    normed = rms_normed(entering, gain_row)
    row_count = normed.shape[0]
    most_rows = min(row_count, N_EXPERT * CAP)

    def one_expert(running_total, expert_index):
        hit_mask = picked == expert_index
        row_share = lax.optimization_barrier(jnp.sum(jnp.where(hit_mask, picked_weights, jnp.float32(0.0)), axis=1))
        live_rows = jnp.any(hit_mask, axis=1)
        live_count = jnp.sum(live_rows.astype(jnp.int32))
        chosen, = jnp.nonzero(live_rows, size=most_rows, fill_value=0)
        valid_rows = (jnp.arange(most_rows, dtype=jnp.int32) < live_count).astype(jnp.float32)
        selected = normed[chosen]
        expert_out = jnp.zeros((most_rows, normed.shape[1]), jnp.float32)
        for shard_index in range(SHARDS):
            slice_index = expert_index * SHARDS + shard_index
            gate_slice = lax.dynamic_index_in_dim(gate_slices, slice_index, 0, keepdims=False)
            down_slice = lax.dynamic_index_in_dim(down_slices, slice_index, 0, keepdims=False)
            projected = jnp.dot(selected, gate_slice, preferred_element_type=jnp.float32)
            hidden_units = (jax.nn.silu(projected[:, :FF_DEV]) * projected[:, FF_DEV:]).astype(jnp.bfloat16)
            partial_out = jnp.dot(hidden_units, down_slice, preferred_element_type=jnp.float32)
            expert_out = expert_out + rounded_back(partial_out)
        contribution = (row_share[chosen] * valid_rows)[:, None] * expert_out
        return (running_total.at[chosen].add(contribution), None)
    running_total = jnp.zeros(values.shape, jnp.float32)
    running_total, _ = lax.scan(one_expert, running_total, jnp.arange(EXPERTS, dtype=jnp.int32))
    return (values + running_total).astype(jnp.bfloat16)

def reference(micro_inputs, norm_gain, gate_up, down_proj, routes, route_weights):
    previous = []
    tick_list = []
    for tick_index in range(TICKS):
        produced = []
        for layer_index in range(LAYERS):
            if layer_index == 0:
                entering = micro_inputs[tick_index]
            elif tick_index == 0:
                entering = micro_inputs[LAYERS + layer_index - 1]
            else:
                entering = previous[layer_index - 1]
            layer_out = moe_layer(entering, norm_gain[layer_index], gate_up[layer_index], down_proj[layer_index], routes[layer_index, tick_index], route_weights[layer_index, tick_index])
            produced.append(layer_out)
        previous = produced
        tick_list.append(jnp.stack(produced))
    return jnp.stack(tick_list, axis=1)
```

```python
import numpy as np
import jax
import jax.numpy as jnp
from jax import lax
from jax.experimental import pallas as pl
from jax.experimental.pallas import tpu as pltpu
from jax.sharding import PartitionSpec as P

D = 3584
FF = 128
N = 8
ROWS = 4
CAP = 2
SLOT = N * CAP
CA = 512
CB = 384
WA = 4 * CA
EPSILON = 1e-06
MESH = pl.DeviceIdType.MESH
ORDER = (4, 3, 5, 2, 6, 1, 7)
BF = jnp.bfloat16
F32 = jnp.float32


def dot(a, b):
    return jnp.dot(a, b, preferred_element_type=F32)


def kernel(ent, gain, wg, wd, la, ra, lb, rb, wslot, perm, out,
           hop, na, nb, sa, sb, ba_send, bb_send, ba, bb,
           pa_send, pb_send, pa, pb, qa_send, qb_send, qa, qb, ssem, rsem, hs, hr):
    s = lax.axis_index("section")
    e = lax.axis_index("expert")
    z, y = e // N, e % N

    def on_z(d):
        return (s, ((z + d) % N) * N + y)

    def on_y(d):
        return (s, z * N + (y + d) % N)

    bar = pltpu.get_barrier_semaphore()
    for d in range(1, N):
        pl.semaphore_signal(bar, inc=1, device_id=on_z(d), device_id_type=MESH)
        pl.semaphore_signal(bar, inc=1, device_id=on_y(d), device_id_type=MESH)
    pl.semaphore_signal(bar, inc=1, device_id=((s + 1) % N, e), device_id_type=MESH)
    pl.semaphore_signal(bar, inc=1, device_id=((s + N - 1) % N, e), device_id_type=MESH)
    pl.semaphore_wait(bar, 2 * (N - 1) + 2)

    def to_peer(phase, d, src, dst, me, along):
        return pltpu.make_async_remote_copy(
            src_ref=src, dst_ref=dst.at[me], send_sem=ssem.at[phase, d], recv_sem=rsem.at[phase, d],
            device_id=along(d), device_id_type=MESH)

    def from_peer(phase, d, src, dst, me, along):
        return pltpu.make_async_remote_copy(
            src_ref=src, dst_ref=dst.at[(me + N - d) % N], send_sem=ssem.at[phase, d],
            recv_sem=rsem.at[phase, d], device_id=along(d), device_id_type=MESH)

    def hop_copy(t):
        return pltpu.make_async_remote_copy(
            src_ref=out.at[t], dst_ref=hop.at[t + 1], send_sem=hs.at[t], recv_sem=hr.at[t],
            device_id=((s + 1) % N, e), device_id_type=MESH)

    phases = (
        (lambda d: na, sa, z, on_z),
        (lambda d: nb, sb, y, on_y),
        (lambda d: ba_send, ba, y, on_y),
        (lambda d: bb_send.at[(z + d) % N], bb, z, on_z),
        (lambda d: pa_send.at[(y + d) % N], pa, y, on_y),
        (lambda d: pb_send.at[(z + d) % N], pb, z, on_z),
        (lambda d: qa_send.at[(z + d) % N], qa, z, on_z),
        (lambda d: qb_send.at[(y + d) % N], qb, y, on_y),
    )

    def start(phase):
        src, dst, me, along = phases[phase]
        for d in ORDER:
            to_peer(phase, d, src(d), dst, me, along).start()

    def arrive(phase):
        src, dst, me, along = phases[phase]
        for d in ORDER:
            from_peer(phase, d, src(d), dst, me, along).wait_recv()

    def sent(phase):
        src, dst, me, along = phases[phase]
        for d in ORDER:
            to_peer(phase, d, src(d), dst, me, along).wait_send()

    def tick(t, carry):
        @pl.when(jnp.logical_or(s == 0, t == 0))
        def _():
            out[t] = ent[t]

        @pl.when(jnp.logical_and(s > 0, t > 0))
        def _():
            hop_copy(t - 1).wait_recv()
            out[t] = hop[t]

        x = out[t].astype(F32)
        ss = jnp.sum(x * x, axis=1, keepdims=True)
        ss = ss + pltpu.roll(ss, 8, 0)
        ss = ss + pltpu.roll(ss, 4, 0)
        n = ((x * lax.rsqrt(ss * (1.0 / D) + EPSILON)) * gain[...]).astype(BF)
        na[...] = n[:, :CA]
        nb[...] = n[:, CA:]
        start(0)
        start(1)
        sa[z] = n[:, :CA]
        sb[y] = n[:, CA:]
        arrive(0)
        ba_send[...] = dot(la[t], sa[...].reshape(128, CA)).astype(BF)
        start(2)
        ba[y] = ba_send[...]
        arrive(1)
        bb_send[...] = dot(lb[t], sb[...].reshape(128, CB)).astype(BF).reshape(N, 64, CB)
        start(3)
        bb[z] = bb_send[z]
        arrive(3)
        proj_b = jnp.zeros((128, 2 * FF), F32)
        for q in range(4):
            proj_b += dot(bb[:, 16 * q:16 * q + 16, :].reshape(128, CB),
                          wg[WA + q * CB:WA + (q + 1) * CB, :])
        high = proj_b.astype(BF)
        low = (proj_b - high.astype(F32)).astype(BF)
        proj = dot(perm[...], high) + dot(perm[...], low)
        arrive(2)
        for q in range(4):
            proj += dot(ba[:, 16 * q:16 * q + 16, :].reshape(128, CA),
                        wg[q * CA:(q + 1) * CA, :])
        gate, up = proj[:, :FF], proj[:, FF:]
        inner = (gate / (1.0 + jnp.exp(-gate)) * up * wslot[t]).astype(BF)
        for q in range(4):
            pa_send[:, 16 * q:16 * q + 16, :] = dot(
                inner, wd[:, q * CA:(q + 1) * CA]).astype(BF).reshape(N, 16, CA)
        start(4)
        inner_b = dot(perm[...], inner).astype(BF)
        for q in range(4):
            pb_send[:, 16 * q:16 * q + 16, :] = dot(
                inner_b, wd[:, WA + q * CB:WA + (q + 1) * CB]).astype(BF).reshape(N, 16, CB)
        start(5)
        pa[y] = pa_send[y]
        pb[z] = pb_send[z]
        arrive(5)
        qb_send[...] = dot(rb[t], pb[...].reshape(512, CB)).astype(BF).reshape(N, 16, CB)
        start(7)
        qb[y] = qb_send[y]
        arrive(4)
        total = pa[0].astype(F32)
        for i in range(1, N):
            total += pa[i].astype(F32)
        qa_send[...] = dot(ra[t], total.astype(BF)).astype(BF).reshape(N, 16, CA)
        start(6)
        qa[z] = qa_send[z]
        arrive(7)
        total_b = qb[0].astype(F32)
        for i in range(1, N):
            total_b += qb[i].astype(F32)
        arrive(6)
        total_a = qa[0].astype(F32)
        for i in range(1, N):
            total_a += qa[i].astype(F32)
        out[t, :, :CA] = (x[:, :CA] + total_a).astype(BF)
        out[t, :, CA:] = (x[:, CA:] + total_b).astype(BF)

        @pl.when(jnp.logical_and(s < N - 1, t < N - 1))
        def _():
            hop_copy(t).start()

        for phase in range(8):
            sent(phase)
        return carry

    lax.fori_loop(0, N, tick, 0)

    @pl.when(s < N - 1)
    def _():
        for t in range(N - 1):
            hop_copy(t).wait_send()


def folded(rows):
    lead = rows.shape[:-2]
    count = rows.shape[-2]
    axes = tuple(range(len(lead))) + (len(lead) + 1, len(lead), len(lead) + 2)
    part_a = rows[..., :WA].reshape(lead + (count, 4, CA)).transpose(axes)
    part_b = rows[..., WA:].reshape(lead + (count, 4, CB)).transpose(axes)
    return jnp.concatenate([part_a, part_b], axis=-1).reshape(lead + (4 * count, CA + CB))


def unfolded(blocks):
    lead = blocks.shape[:-2]
    axes = tuple(range(len(lead))) + (len(lead) + 1, len(lead), len(lead) + 2)
    split = blocks.reshape(lead + (4, ROWS, CA + CB)).transpose(axes)
    return jnp.concatenate([split[..., :CA].reshape(lead + (ROWS, WA)),
                            split[..., CA:].reshape(lead + (ROWS, D - WA))], axis=-1)


def slot_weights(picked, weights):
    flat = picked.reshape(N, -1)
    order = jnp.arange(flat.shape[1])
    earlier = (flat[:, None, :] == flat[:, :, None]) & (order[None, None, :] < order[None, :, None])
    place = jnp.sum(earlier.astype(jnp.int32), axis=2).reshape(picked.shape)
    slot = picked * CAP + place
    hit = slot[..., None] == jnp.arange(N * CAP)
    return jnp.sum(jnp.where(hit, weights[..., None], 0.0), axis=2)


def body(micro_inputs, norm_gain, gate_up, down_proj, routes, route_weights):
    s = lax.axis_index("section")
    e = lax.axis_index("expert")
    z, y = e // N, e % N
    first = lax.dynamic_index_in_dim(micro_inputs, jnp.where(s == 0, 0, N - 1 + s), 0, keepdims=True)
    ent = folded(jnp.concatenate([first, micro_inputs[1:N]], axis=0))
    gain = folded(jnp.broadcast_to(norm_gain[0].astype(F32), (ROWS, D)))

    own = slot_weights(routes[0], route_weights[0])
    every = lax.all_gather(own, "expert").reshape(N, N, N, ROWS, N, CAP)
    eye8 = jnp.eye(N, dtype=BF)
    eye4 = jnp.eye(4, dtype=BF)
    column = lax.dynamic_index_in_dim(every, y, 1, keepdims=False)
    hits_a = (lax.dynamic_index_in_dim(column, z, 3, keepdims=False) > 0).astype(BF)
    la = jnp.einsum("ztrc,zw,qp->tqzcwpr", hits_a, eye8, eye4).reshape(N, 64, 128)
    hits_b = (lax.dynamic_index_in_dim(every, z, 0, keepdims=False) > 0).astype(BF)
    lb = jnp.einsum("ytrec,yw,qp->teqycwpr", hits_b, eye8, eye4).reshape(N, 512, 128)
    mine = lax.dynamic_index_in_dim(every, z, 4, keepdims=False)
    wslot = jnp.sum(mine, axis=3).transpose(2, 1, 0, 3).reshape(N, 128, 1)
    wslot = jnp.broadcast_to(wslot, (N, 128, 128))
    index = np.arange(128)
    swapped = (index // 2 % 8) * 16 + index // 16 * 2 + index % 2
    perm = jnp.asarray(swapped[:, None] == index[None, :], BF)

    vmem = pl.BlockSpec(memory_space=pltpu.VMEM)
    out = pl.pallas_call(
        kernel,
        out_shape=jax.ShapeDtypeStruct((N, 16, CA + CB), BF),
        in_specs=[vmem] * 10,
        out_specs=vmem,
        scratch_shapes=[
            pltpu.VMEM((N, 16, CA + CB), BF),
            pltpu.VMEM((16, CA), BF), pltpu.VMEM((16, CB), BF),
            pltpu.VMEM((N, 16, CA), BF), pltpu.VMEM((N, 16, CB), BF),
            pltpu.VMEM((64, CA), BF), pltpu.VMEM((N, 64, CB), BF),
            pltpu.VMEM((N, 64, CA), BF), pltpu.VMEM((N, 64, CB), BF),
            pltpu.VMEM((N, 64, CA), BF), pltpu.VMEM((N, 64, CB), BF),
            pltpu.VMEM((N, 64, CA), BF), pltpu.VMEM((N, 64, CB), BF),
            pltpu.VMEM((N, 16, CA), BF), pltpu.VMEM((N, 16, CB), BF),
            pltpu.VMEM((N, 16, CA), BF), pltpu.VMEM((N, 16, CB), BF),
            pltpu.SemaphoreType.DMA((8, N)), pltpu.SemaphoreType.DMA((8, N)),
            pltpu.SemaphoreType.DMA((N,)), pltpu.SemaphoreType.DMA((N,)),
        ],
        compiler_params=pltpu.CompilerParams(
            collective_id=0, has_side_effects=True, vmem_limit_bytes=40 << 20),
    )(ent, gain, gate_up[0, 0], down_proj[0, 0], la, la.transpose(0, 2, 1), lb,
      lb.transpose(0, 2, 1), wslot, perm)
    return unfolded(out)[None]


def solution(mesh):
    return jax.shard_map(
        body,
        mesh=mesh,
        in_specs=(
            P(None, "expert", None),
            P("section", None),
            P("section", "expert", None, None),
            P("section", "expert", None, None),
            P("section", None, "expert", None),
            P("section", None, "expert", None),
        ),
        out_specs=P("section", None, "expert", None),
        check_vma=False,
    )
```

```python
import numpy as np
import jax
import jax.numpy as jnp
from jax import lax
from jax.experimental import pallas as pl
from jax.experimental.pallas import tpu as pltpu
from jax.sharding import PartitionSpec as P

D = 3584
FF = 128
N = 8
ROWS = 4
CAP = 2
CA = 512
CB = 384
WA = 4 * CA
NB = 2
G = N // NB
SL = G * CAP
GR = G * 16
BLK = 4 * SL
EPSILON = 1e-06
MESH = pl.DeviceIdType.MESH
ORDER = (4, 3, 5, 2, 6, 1, 7)
BF = jnp.bfloat16
F32 = jnp.float32


def dot(a, b):
    return jnp.dot(a, b, preferred_element_type=F32)


def dot_t(a, b):
    return lax.dot_general(a, b, (((1,), (1,)), ((), ())), preferred_element_type=F32)


def exact(a, b):
    return jnp.dot(a, b, preferred_element_type=F32, precision=lax.Precision.HIGHEST)


def kernel(ent, gain, hown, wg_hbm, wd_hbm, e1, gt, mt, ma, mb, perm, sw, out,
           wg, wd, hop, hz, hy, hzt, hyt, wsend, wbuf, la, lb, ra, rb,
           na, nb, sa, sb, ba_send, bb_send, ba, bb, pa_send, pb_send, pa, pb,
           qa_send, qb_send, qa, qb, ssem, rsem, s1, r1, hs, hr, wsem):
    s = lax.axis_index("section")
    e = lax.axis_index("expert")
    z, y = e // N, e % N
    mine = (z + y) % NB

    def on_z(d):
        return (s, ((z + d) % N) * N + y)

    def on_y(d):
        return (s, z * N + (y + d) % N)

    load_g = pltpu.make_async_copy(wg_hbm.at[0, 0], wg, wsem.at[0])
    load_d = pltpu.make_async_copy(wd_hbm.at[0, 0], wd, wsem.at[1])
    load_g.start()
    load_d.start()

    bar = pltpu.get_barrier_semaphore()
    for d in range(1, N):
        pl.semaphore_signal(bar, inc=1, device_id=on_z(d), device_id_type=MESH)
        pl.semaphore_signal(bar, inc=1, device_id=on_y(d), device_id_type=MESH)
    pl.semaphore_signal(bar, inc=1, device_id=((s + 1) % N, e), device_id_type=MESH)
    pl.semaphore_signal(bar, inc=1, device_id=((s + N - 1) % N, e), device_id_type=MESH)
    pl.semaphore_wait(bar, 2 * (N - 1) + 2)

    def remote(phase, h, d, src, dst, target):
        return pltpu.make_async_remote_copy(
            src_ref=src, dst_ref=dst, send_sem=ssem.at[phase, h, d], recv_sem=rsem.at[phase, h, d],
            device_id=target, device_id_type=MESH)

    def once(phase, d, src, dst, target):
        return pltpu.make_async_remote_copy(
            src_ref=src, dst_ref=dst, send_sem=s1.at[phase, d], recv_sem=r1.at[phase, d],
            device_id=target, device_id_type=MESH)

    def at(v):
        return (v % NB) * G + v // NB

    def table_copies(d, back):
        zz, yy = ((z + N - d) % N, (y + N - d) % N) if back else (z, y)
        return (once(0, d, hown, hz.at[at(zz)], on_z(d)), once(1, d, hown, hy.at[at(yy)], on_y(d)))

    def weight_copy(d, back):
        return once(2, d, wsend, wbuf.at[(y + N - d) % N if back else y], on_y(d))

    def small_a(h, d, back):
        return remote(0, h, d, na, sa.at[h, ((z + N - d) % N if back else z) // NB], on_z(d))

    def small_b(h, d, back):
        return remote(1, h, d, nb, sb.at[h, ((y + N - d) % N if back else y) // NB], on_y(d))

    def big_a(h, d, back):
        return remote(2, h, d, ba_send.at[h], ba.at[h, (y + N - d) % N if back else y], on_y(d))

    def big_b(h, d, back):
        return remote(3, h, d, bb_send.at[h, (z + d) % N], bb.at[h, (z + N - d) % N if back else z],
                      on_z(d))

    def ret_a(h, d, back):
        return remote(4, h, d, pa_send.at[h, (y + d) % N], pa.at[h, (y + N - d) % N if back else y],
                      on_y(d))

    def ret_b(h, d, back):
        return remote(5, h, d, pb_send.at[h, (z + d) % N], pb.at[h, (z + N - d) % N if back else z],
                      on_z(d))

    def home_a(h, d, back):
        return remote(6, h, d, qa_send.at[h, ((z + d) % N) // NB],
                      qa.at[(z + N - d) % N if back else z], on_z(d))

    def home_b(h, d, back):
        return remote(7, h, d, qb_send.at[h, ((y + d) % N) // NB],
                      qb.at[(y + N - d) % N if back else y], on_y(d))

    def hop_copy(t):
        return pltpu.make_async_remote_copy(
            src_ref=out.at[t], dst_ref=hop.at[t + 1], send_sem=hs.at[t], recv_sem=hr.at[t],
            device_id=((s + 1) % N, e), device_id_type=MESH)

    def each_source(h, act):
        first = (mine + NB - h) % NB
        for k in range(G - 1, 0, -1):
            act(k * NB + first)

        @pl.when(first != 0)
        def _():
            act(first)

    def each_home(h, act):
        first = (h + NB - mine) % NB
        for k in range(G - 1, 0, -1):
            act(k * NB + first)

        @pl.when(first != 0)
        def _():
            act(first)

    def spread_hits(h, t):
        from_z = pl.multiple_of(((h + N - y) % NB) * (G * 8), G * 8)
        from_y = pl.multiple_of(((h + N - z) % NB) * (G * 8), G * 8)
        xz = dot(e1[...], hzt[t, pl.ds(from_z, G * 8), :]).astype(BF)
        xy = dot(e1[...], hyt[t, pl.ds(from_y, G * 8), :]).astype(BF)
        return xz, xy, gt[pl.ds(pl.multiple_of(z * BLK, BLK), BLK), :]

    def begin(h, t):
        @pl.when(mine == h)
        def _():
            @pl.when(jnp.logical_or(s == 0, t == 0))
            def _():
                out[t] = ent[t]

            @pl.when(jnp.logical_and(s > 0, t > 0))
            def _():
                hop_copy(t - 1).wait_recv()
                out[t] = hop[t]

            x = out[t].astype(F32)
            ss = jnp.sum(x * x, axis=1, keepdims=True)
            ss = ss + pltpu.roll(ss, 8, 0)
            ss = ss + pltpu.roll(ss, 4, 0)
            n = ((x * lax.rsqrt(ss * (1.0 / D) + EPSILON)) * gain[...]).astype(BF)
            na[...] = n[:, :CA]
            nb[...] = n[:, CA:]
            for d in ORDER:
                small_a(h, d, False).start()
                small_b(h, d, False).start()
            sa[h, z // NB] = n[:, :CA]
            sb[h, y // NB] = n[:, CA:]

        if h == 0:
            @pl.when(t == 0)
            def _():
                for d in ORDER:
                    for c in table_copies(d, True):
                        c.wait_recv()
                all_z = hz[...].reshape(64, 128)
                all_y = hy[...].reshape(64, 128)
                for i in range(N):
                    hzt[i] = jnp.where(pltpu.roll(all_z, (128 - 16 * i) % 128, 1) > 0, 1.0, 0.0).astype(BF)
                    hyt[i] = jnp.where(pltpu.roll(all_y, (128 - 16 * i) % 128, 1) > 0, 1.0, 0.0).astype(BF)
                lane = lax.broadcasted_iota(jnp.int32, (128, 128), 0)
                tick_of = lax.broadcasted_iota(jnp.int32, (128, 128), 1)
                pick = jnp.where((lane // 16 == tick_of) & ((lane // 2) % N == z), 1.0, 0.0)
                odd = lax.broadcasted_iota(jnp.int32, (SL, 128), 1) % 2
                row = lax.broadcasted_iota(jnp.int32, (SL, 128), 0) % 2
                for g in range(NB):
                    sums = exact(sw[...], hz[pl.ds(((g + N - y) % NB) * G, G)].reshape(G * 8, 128))
                    wsend[g * SL:(g + 1) * SL, :] = exact(jnp.where(odd == row, sums, 0.0), pick)
                for d in ORDER:
                    weight_copy(d, False).start()
                wbuf[y] = wsend[...]

        xz, xy, gz = spread_hits(h, t)
        la[h] = (dot_t(gz, xz) * mt[...]).astype(BF)
        lb[h] = (dot_t(gt[...], xy).reshape(N, BLK, GR) * mt[...][None]).reshape(N * BLK, GR).astype(BF)

    def select(h, t):
        each_source(h, lambda d: small_a(h, d, True).wait_recv())
        ba_send[h] = dot(la[h], sa[h].reshape(GR, CA)).astype(BF)
        for d in ORDER:
            big_a(h, d, False).start()
        ba[h, y] = ba_send[h]
        each_source(h, lambda d: small_b(h, d, True).wait_recv())
        bb_send[h] = dot(lb[h], sb[h].reshape(GR, CB)).astype(BF).reshape(N, BLK, CB)
        for d in ORDER:
            big_b(h, d, False).start()
        bb[h, z] = bb_send[h, z]

    def quarter(block, q, columns):
        return block[:, SL * q:SL * q + SL, :].reshape(N * SL, columns).astype(BF)

    def outward(rows, first, columns):
        parts = [dot(rows, wd[:, first + q * columns:first + (q + 1) * columns]).reshape(N, SL, columns)
                 for q in range(4)]
        return jnp.concatenate(parts, axis=1).astype(BF)

    def experts(h, t):
        if h == 0:
            @pl.when(t == 0)
            def _():
                load_g.wait()
                load_d.wait()
                for d in ORDER:
                    weight_copy(d, True).wait_recv()
        for d in ORDER:
            big_b(h, d, True).wait_recv()
        rows_b = bb[h].astype(F32)
        proj_b = jnp.zeros((N * SL, 2 * FF), F32)
        for q in range(4):
            proj_b += dot(quarter(rows_b, q, CB), wg[WA + q * CB:WA + (q + 1) * CB, :])
        high = proj_b.astype(BF)
        low = (proj_b - high.astype(F32)).astype(BF)
        proj = dot(perm[h], high) + dot(perm[h], low)
        tick_lane = lax.broadcasted_iota(jnp.int32, (N * SL, 128), 1) == t
        weight = jnp.sum(jnp.where(tick_lane, wbuf[:, SL * h:SL * h + SL, :].reshape(N * SL, 128), 0.0),
                         axis=1, keepdims=True)
        for d in ORDER:
            big_a(h, d, True).wait_recv()
        rows_a = ba[h].astype(F32)
        for q in range(4):
            proj += dot(quarter(rows_a, q, CA), wg[q * CA:(q + 1) * CA, :])
        gate, up = proj[:, :FF], proj[:, FF:]
        inner = (gate / (1.0 + jnp.exp(-gate)) * up * weight).astype(BF)
        pa_send[h] = outward(inner, 0, CA)
        for d in ORDER:
            ret_a(h, d, False).start()
        pb_send[h] = outward(dot(perm[h], inner).astype(BF), WA, CB)
        for d in ORDER:
            ret_b(h, d, False).start()
        pa[h, y] = pa_send[h, y]
        pb[h, z] = pb_send[h, z]
        xz, xy, gz = spread_hits(h, t)
        ra[h] = (dot_t(xz, gz) * ma[...]).astype(BF)
        rb[h] = (dot_t(xy, gt[...]) * mb[...]).astype(BF)

        @pl.when(mine == h)
        def _():
            for d in ORDER:
                small_a(h, d, False).wait_send()
                small_b(h, d, False).wait_send()

    def gather(h, t):
        @pl.when(t > 0)
        def _():
            each_home(h, lambda d: (home_a(h, d, False).wait_send(), home_b(h, d, False).wait_send()))
        for d in ORDER:
            ret_b(h, d, True).wait_recv()
        qb_send[h] = dot(rb[h], pb[h].reshape(N * BLK, CB)).astype(BF).reshape(G, 16, CB)
        each_home(h, lambda d: home_b(h, d, False).start())
        for d in ORDER:
            ret_a(h, d, True).wait_recv()
        total = pa[h, 0].astype(F32)
        for i in range(1, N):
            total += pa[h, i].astype(F32)
        qa_send[h] = dot(ra[h], total.astype(BF)).astype(BF).reshape(G, 16, CA)
        each_home(h, lambda d: home_a(h, d, False).start())
        for d in ORDER:
            big_a(h, d, False).wait_send()
            big_b(h, d, False).wait_send()
            ret_a(h, d, False).wait_send()
            ret_b(h, d, False).wait_send()

    def finish(h, t):
        @pl.when(mine == h)
        def _():
            qa[z] = qa_send[h, z // NB]
            qb[y] = qb_send[h, y // NB]
            x = out[t].astype(F32)
            for d in ORDER:
                home_b(h, d, True).wait_recv()
            total_b = qb[0].astype(F32)
            for i in range(1, N):
                total_b += qb[i].astype(F32)
            for d in ORDER:
                home_a(h, d, True).wait_recv()
            total_a = qa[0].astype(F32)
            for i in range(1, N):
                total_a += qa[i].astype(F32)
            out[t, :, :CA] = (x[:, :CA] + total_a).astype(BF)
            out[t, :, CA:] = (x[:, CA:] + total_b).astype(BF)

            @pl.when(jnp.logical_and(s < N - 1, t < N - 1))
            def _():
                hop_copy(t).start()

    for d in ORDER:
        for c in table_copies(d, False):
            c.start()
    hz[at(z)] = hown[...]
    hy[at(y)] = hown[...]

    if NB == 1:
        def tick(t, carry):
            for stage in (begin, select, experts, gather, finish):
                stage(0, t)
            return carry

        lax.fori_loop(0, N, tick, 0)
    else:
        def tick(t, carry):
            @pl.when(t < N)
            def _():
                begin(0, t)
                select(0, t)

            @pl.when(t > 0)
            def _():
                gather(1, t - 1)
                finish(1, t - 1)

            @pl.when(t < N)
            def _():
                experts(0, t)
                begin(1, t)
                select(1, t)
                gather(0, t)
                finish(0, t)
                experts(1, t)
            return carry

        lax.fori_loop(0, N + 1, tick, 0)

    for h in range(NB):
        each_home(h, lambda d: (home_a(h, d, False).wait_send(), home_b(h, d, False).wait_send()))
    for d in ORDER:
        for c in table_copies(d, False):
            c.wait_send()
        weight_copy(d, False).wait_send()

    @pl.when(s < N - 1)
    def _():
        for t in range(N - 1):
            hop_copy(t).wait_send()


def folded(rows):
    lead = rows.shape[:-2]
    count = rows.shape[-2]
    axes = tuple(range(len(lead))) + (len(lead) + 1, len(lead), len(lead) + 2)
    part_a = rows[..., :WA].reshape(lead + (count, 4, CA)).transpose(axes)
    part_b = rows[..., WA:].reshape(lead + (count, 4, CB)).transpose(axes)
    return jnp.concatenate([part_a, part_b], axis=-1).reshape(lead + (4 * count, CA + CB))


def unfolded(blocks):
    lead = blocks.shape[:-2]
    axes = tuple(range(len(lead))) + (len(lead) + 1, len(lead), len(lead) + 2)
    split = blocks.reshape(lead + (4, ROWS, CA + CB)).transpose(axes)
    return jnp.concatenate([split[..., :CA].reshape(lead + (ROWS, WA)),
                            split[..., CA:].reshape(lead + (ROWS, D - WA))], axis=-1)


def slot_weights(picked, weights):
    flat = picked.reshape(N, -1)
    order = jnp.arange(flat.shape[1])
    earlier = (flat[:, None, :] == flat[:, :, None]) & (order[None, None, :] < order[None, :, None])
    place = jnp.sum(earlier.astype(jnp.int32), axis=2).reshape(picked.shape)
    slot = picked * CAP + place
    hit = slot[..., None] == jnp.arange(N * CAP)
    return jnp.sum(jnp.where(hit, weights[..., None], 0.0), axis=2)


def constants():
    e1 = np.zeros((G, 4, ROWS, G, 8), np.float32)
    for i in range(G):
        for r in range(ROWS):
            e1[i, :, r, i, r] = 1
    gt = np.zeros((N, 4, G, CAP, 128), np.float32)
    for k in range(N):
        for c in range(CAP):
            gt[k, :, :, c, k * CAP + c] = 1
    mt = np.zeros((4, G, CAP, G, 4, ROWS), np.float32)
    for q in range(4):
        for i in range(G):
            mt[q, i, :, i, q, :] = 1
    mt = mt.reshape(BLK, GR)
    sw = np.zeros((G, CAP, G, 8), np.float32)
    for i in range(G):
        sw[i, :, i, :ROWS] = 1
    perm = np.zeros((NB, N * SL, N * SL), np.float32)
    for k in range(N):
        for j in range(N):
            for c in range(CAP):
                perm[(k + j) % NB, j * SL + k // NB * CAP + c, k * SL + j // NB * CAP + c] = 1
    return (jnp.asarray(e1.reshape(GR, G * 8), BF), jnp.asarray(gt.reshape(N * BLK, 128), BF),
            jnp.asarray(mt), jnp.asarray(mt.T), jnp.asarray(np.tile(mt.T, (1, N))),
            jnp.asarray(perm, BF), jnp.asarray(sw.reshape(SL, G * 8)))


def body(micro_inputs, norm_gain, gate_up, down_proj, routes, route_weights):
    s = lax.axis_index("section")
    first = lax.dynamic_index_in_dim(micro_inputs, jnp.where(s == 0, 0, N - 1 + s), 0, keepdims=True)
    ent = folded(jnp.concatenate([first, micro_inputs[1:N]], axis=0))
    gain = folded(jnp.broadcast_to(norm_gain[0].astype(F32), (ROWS, D)))
    own = slot_weights(routes[0], route_weights[0]).transpose(1, 0, 2).reshape(ROWS, 128)
    own = jnp.concatenate([own, jnp.zeros_like(own)], axis=0)

    vmem = pl.BlockSpec(memory_space=pltpu.VMEM)
    hbm = pl.BlockSpec(memory_space=pl.ANY)
    out = pl.pallas_call(
        kernel,
        out_shape=jax.ShapeDtypeStruct((N, 16, CA + CB), BF),
        in_specs=[vmem] * 3 + [hbm] * 2 + [vmem] * 7,
        out_specs=vmem,
        scratch_shapes=[
            pltpu.VMEM((D, 2 * FF), BF), pltpu.VMEM((FF, D), BF),
            pltpu.VMEM((N, 16, CA + CB), BF),
            pltpu.VMEM((N, 8, 128), F32), pltpu.VMEM((N, 8, 128), F32),
            pltpu.VMEM((N, 64, 128), BF), pltpu.VMEM((N, 64, 128), BF),
            pltpu.VMEM((16, 128), F32), pltpu.VMEM((N, 16, 128), F32),
            pltpu.VMEM((NB, BLK, GR), BF), pltpu.VMEM((NB, N * BLK, GR), BF),
            pltpu.VMEM((NB, GR, BLK), BF), pltpu.VMEM((NB, GR, N * BLK), BF),
            pltpu.VMEM((16, CA), BF), pltpu.VMEM((16, CB), BF),
            pltpu.VMEM((NB, G, 16, CA), BF), pltpu.VMEM((NB, G, 16, CB), BF),
            pltpu.VMEM((NB, BLK, CA), BF), pltpu.VMEM((NB, N, BLK, CB), BF),
            pltpu.VMEM((NB, N, BLK, CA), BF), pltpu.VMEM((NB, N, BLK, CB), BF),
            pltpu.VMEM((NB, N, BLK, CA), BF), pltpu.VMEM((NB, N, BLK, CB), BF),
            pltpu.VMEM((NB, N, BLK, CA), BF), pltpu.VMEM((NB, N, BLK, CB), BF),
            pltpu.VMEM((NB, G, 16, CA), BF), pltpu.VMEM((NB, G, 16, CB), BF),
            pltpu.VMEM((N, 16, CA), BF), pltpu.VMEM((N, 16, CB), BF),
            pltpu.SemaphoreType.DMA((8, NB, N)), pltpu.SemaphoreType.DMA((8, NB, N)),
            pltpu.SemaphoreType.DMA((3, N)), pltpu.SemaphoreType.DMA((3, N)),
            pltpu.SemaphoreType.DMA((N,)), pltpu.SemaphoreType.DMA((N,)),
            pltpu.SemaphoreType.DMA((2,)),
        ],
        compiler_params=pltpu.CompilerParams(
            collective_id=0, has_side_effects=True, vmem_limit_bytes=40 << 20),
    )(ent, gain, own, gate_up, down_proj, *constants())
    return unfolded(out)[None]


def solution(mesh):
    return jax.shard_map(
        body,
        mesh=mesh,
        in_specs=(
            P(None, "expert", None),
            P("section", None),
            P("section", "expert", None, None),
            P("section", "expert", None, None),
            P("section", None, "expert", None),
            P("section", None, "expert", None),
        ),
        out_specs=P("section", None, "expert", None),
        check_vma=False,
    )
```

```python
import numpy as np
import jax
import jax.numpy as jnp
from jax import lax
from jax.experimental import pallas as pl
from jax.experimental.pallas import tpu as pltpu
from jax.sharding import PartitionSpec as P

D = 3584
FF = 128
N = 8
ROWS = 4
CAP = 2
CA = 512
CB = 384
WA = 4 * CA
NB = 2
G = N // NB
SL = G * CAP
GR = G * 16
BLK = 4 * SL
EPSILON = 1e-06
MESH = pl.DeviceIdType.MESH
ORDER = (4, 3, 5, 2, 6, 1, 7)
BF = jnp.bfloat16
F32 = jnp.float32


def dot(a, b):
    return jnp.dot(a, b, preferred_element_type=F32)


def dot_t(a, b):
    return lax.dot_general(a, b, (((1,), (1,)), ((), ())), preferred_element_type=F32)


def exact(a, b):
    return jnp.dot(a, b, preferred_element_type=F32, precision=lax.Precision.HIGHEST)


def folded(x):
    part_a = jnp.concatenate([x[:, q * CA:(q + 1) * CA] for q in range(4)], axis=0)
    part_b = jnp.concatenate([x[:, WA + q * CB:WA + (q + 1) * CB] for q in range(4)], axis=0)
    return jnp.concatenate([part_a, part_b], axis=1)


def kernel(micro, norm_gain, picked, weights, wg_hbm, wd_hbm, e1, gt, mt, ma, mb, perm, sw, out,
           gain, hown, wg, wd, hop, hz, hy, hzt, hyt, wsend, wbuf, la, lb, ra, rb,
           na, nb, sa, sb, ba_send, bb_send, ba, bb, pa_send, pb_send, pa, pb,
           qa_send, qb_send, qa, qb, ssem, rsem, s1, r1, hs, hr, wsem):
    s = lax.axis_index("section")
    e = lax.axis_index("expert")
    z, y = e // N, e % N
    mine = (z + y) % NB

    def on_z(d):
        return (s, ((z + d) % N) * N + y)

    def on_y(d):
        return (s, z * N + (y + d) % N)

    load_g = pltpu.make_async_copy(wg_hbm.at[0, 0], wg, wsem.at[0])
    load_d = pltpu.make_async_copy(wd_hbm.at[0, 0], wd, wsem.at[1])
    load_g.start()
    load_d.start()

    gain[...] = folded(jnp.broadcast_to(norm_gain[...].astype(F32), (ROWS, D)))
    lanes = lax.broadcasted_iota(jnp.int32, (8, 128), 1)
    row = lax.broadcasted_iota(jnp.int32, (8, 128), 0)
    expert = (lanes >> 1) & 7
    first_pick, second_pick = picked[0] == expert, picked[1] == expert
    taken = jnp.where(first_pick | second_pick, 1.0, 0.0)
    ahead = jnp.zeros((8, 128), F32)
    for i in range(1, ROWS):
        ahead += jnp.where(row >= i, pltpu.roll(taken, i, 0), 0.0)
    in_place = (ahead == (lanes & 1).astype(F32)) & (taken > 0)
    hown[...] = jnp.where(in_place, jnp.where(first_pick, weights[0], weights[1]), 0.0)

    bar = pltpu.get_barrier_semaphore()
    for d in range(1, N):
        pl.semaphore_signal(bar, inc=1, device_id=on_z(d), device_id_type=MESH)
        pl.semaphore_signal(bar, inc=1, device_id=on_y(d), device_id_type=MESH)
    pl.semaphore_signal(bar, inc=1, device_id=((s + 1) % N, e), device_id_type=MESH)
    pl.semaphore_signal(bar, inc=1, device_id=((s + N - 1) % N, e), device_id_type=MESH)
    pl.semaphore_wait(bar, 2 * (N - 1) + 2)

    def remote(phase, h, d, src, dst, target):
        return pltpu.make_async_remote_copy(
            src_ref=src, dst_ref=dst, send_sem=ssem.at[phase, h, d], recv_sem=rsem.at[phase, h, d],
            device_id=target, device_id_type=MESH)

    def once(phase, d, src, dst, target):
        return pltpu.make_async_remote_copy(
            src_ref=src, dst_ref=dst, send_sem=s1.at[phase, d], recv_sem=r1.at[phase, d],
            device_id=target, device_id_type=MESH)

    def at(v):
        return (v % NB) * G + v // NB

    def table_copies(d, back):
        zz, yy = ((z + N - d) % N, (y + N - d) % N) if back else (z, y)
        return (once(0, d, hown, hz.at[at(zz)], on_z(d)), once(1, d, hown, hy.at[at(yy)], on_y(d)))

    def weight_copy(d, back):
        return once(2, d, wsend, wbuf.at[(y + N - d) % N if back else y], on_y(d))

    def small_a(h, d, back):
        return remote(0, h, d, na, sa.at[h, ((z + N - d) % N if back else z) // NB], on_z(d))

    def small_b(h, d, back):
        return remote(1, h, d, nb, sb.at[h, ((y + N - d) % N if back else y) // NB], on_y(d))

    def big_a(h, d, back):
        return remote(2, h, d, ba_send.at[h], ba.at[h, (y + N - d) % N if back else y], on_y(d))

    def big_b(h, d, back):
        return remote(3, h, d, bb_send.at[h, (z + d) % N], bb.at[h, (z + N - d) % N if back else z],
                      on_z(d))

    def ret_a(h, d, back):
        return remote(4, h, d, pa_send.at[h, (y + d) % N], pa.at[h, (y + N - d) % N if back else y],
                      on_y(d))

    def ret_b(h, d, back):
        return remote(5, h, d, pb_send.at[h, (z + d) % N], pb.at[h, (z + N - d) % N if back else z],
                      on_z(d))

    def home_a(h, d, back):
        return remote(6, h, d, qa_send.at[h, ((z + d) % N) // NB],
                      qa.at[(z + N - d) % N if back else z], on_z(d))

    def home_b(h, d, back):
        return remote(7, h, d, qb_send.at[h, ((y + d) % N) // NB],
                      qb.at[(y + N - d) % N if back else y], on_y(d))

    def hop_copy(t):
        return pltpu.make_async_remote_copy(
            src_ref=out.at[t], dst_ref=hop.at[t + 1], send_sem=hs.at[t], recv_sem=hr.at[t],
            device_id=((s + 1) % N, e), device_id_type=MESH)

    def each_source(h, act):
        first = (mine + NB - h) % NB
        for k in range(G - 1, 0, -1):
            act(k * NB + first)

        @pl.when(first != 0)
        def _():
            act(first)

    def each_home(h, act):
        first = (h + NB - mine) % NB
        for k in range(G - 1, 0, -1):
            act(k * NB + first)

        @pl.when(first != 0)
        def _():
            act(first)

    def spread_hits(h, t):
        from_z = pl.multiple_of(((h + N - y) % NB) * (G * 8), G * 8)
        from_y = pl.multiple_of(((h + N - z) % NB) * (G * 8), G * 8)
        xz = dot(e1[...], hzt[t, pl.ds(from_z, G * 8), :]).astype(BF)
        xy = dot(e1[...], hyt[t, pl.ds(from_y, G * 8), :]).astype(BF)
        return xz, xy, gt[pl.ds(pl.multiple_of(z * BLK, BLK), BLK), :]

    def begin(h, t):
        @pl.when(mine == h)
        def _():
            @pl.when(jnp.logical_or(s == 0, t == 0))
            def _():
                out[t] = folded(micro[t + (s + N - 1) // N * (s + N - 1)].astype(F32)).astype(BF)

            @pl.when(jnp.logical_and(s > 0, t > 0))
            def _():
                hop_copy(t - 1).wait_recv()
                out[t] = hop[t]

            x = out[t].astype(F32)
            ss = jnp.sum(x * x, axis=1, keepdims=True)
            ss = ss + pltpu.roll(ss, 8, 0)
            ss = ss + pltpu.roll(ss, 4, 0)
            n = ((x * lax.rsqrt(ss * (1.0 / D) + EPSILON)) * gain[...]).astype(BF)
            na[...] = n[:, :CA]
            nb[...] = n[:, CA:]
            for d in ORDER:
                small_a(h, d, False).start()
                small_b(h, d, False).start()
            sa[h, z // NB] = n[:, :CA]
            sb[h, y // NB] = n[:, CA:]

        if h == 0:
            @pl.when(t == 0)
            def _():
                for d in ORDER:
                    for c in table_copies(d, True):
                        c.wait_recv()
                all_z = hz[...].reshape(64, 128)
                all_y = hy[...].reshape(64, 128)
                for i in range(N):
                    hzt[i] = jnp.where(pltpu.roll(all_z, (128 - 16 * i) % 128, 1) > 0, 1.0, 0.0).astype(BF)
                    hyt[i] = jnp.where(pltpu.roll(all_y, (128 - 16 * i) % 128, 1) > 0, 1.0, 0.0).astype(BF)
                lane = lax.broadcasted_iota(jnp.int32, (128, 128), 0)
                tick_of = lax.broadcasted_iota(jnp.int32, (128, 128), 1)
                pick = jnp.where((lane // 16 == tick_of) & ((lane // 2) % N == z), 1.0, 0.0)
                odd = lax.broadcasted_iota(jnp.int32, (SL, 128), 1) % 2
                row = lax.broadcasted_iota(jnp.int32, (SL, 128), 0) % 2
                for g in range(NB):
                    sums = exact(sw[...], hz[pl.ds(((g + N - y) % NB) * G, G)].reshape(G * 8, 128))
                    wsend[g * SL:(g + 1) * SL, :] = exact(jnp.where(odd == row, sums, 0.0), pick)
                for d in ORDER:
                    weight_copy(d, False).start()
                wbuf[y] = wsend[...]

        xz, xy, gz = spread_hits(h, t)
        la[h] = (dot_t(gz, xz) * mt[...]).astype(BF)
        lb[h] = (dot_t(gt[...], xy).reshape(N, BLK, GR) * mt[...][None]).reshape(N * BLK, GR).astype(BF)

    def select(h, t):
        each_source(h, lambda d: small_a(h, d, True).wait_recv())
        ba_send[h] = dot(la[h], sa[h].reshape(GR, CA)).astype(BF)
        for d in ORDER:
            big_a(h, d, False).start()
        ba[h, y] = ba_send[h]
        each_source(h, lambda d: small_b(h, d, True).wait_recv())
        bb_send[h] = dot(lb[h], sb[h].reshape(GR, CB)).astype(BF).reshape(N, BLK, CB)
        for d in ORDER:
            big_b(h, d, False).start()
        bb[h, z] = bb_send[h, z]

    def inward(block, first, columns):
        per = 16 // SL
        total = jnp.zeros((N * SL, 2 * FF), F32)
        for q in range(4):
            rows = block[:, q // per * 16:q // per * 16 + 16, :].reshape(N * 16, columns)
            product = dot(rows, wg[first + q * columns:first + (q + 1) * columns, :])
            total += product.reshape(N, per, SL, 2 * FF)[:, q % per].reshape(N * SL, 2 * FF)
        return total

    def outward(rows, first, columns):
        parts = [dot(rows, wd[:, first + q * columns:first + (q + 1) * columns]).reshape(N, SL, columns)
                 for q in range(4)]
        return jnp.concatenate(parts, axis=1).astype(BF)

    def experts(h, t):
        if h == 0:
            @pl.when(t == 0)
            def _():
                load_g.wait()
                load_d.wait()
                for d in ORDER:
                    weight_copy(d, True).wait_recv()
        for d in ORDER:
            big_b(h, d, True).wait_recv()
        proj_b = inward(bb[h], WA, CB)
        high = proj_b.astype(BF)
        low = (proj_b - high.astype(F32)).astype(BF)
        proj = dot(perm[h], high) + dot(perm[h], low)
        tick_lane = lax.broadcasted_iota(jnp.int32, (N * SL, 128), 1) == t
        weight = jnp.sum(jnp.where(tick_lane, wbuf[:, SL * h:SL * h + SL, :].reshape(N * SL, 128), 0.0),
                         axis=1, keepdims=True)
        for d in ORDER:
            big_a(h, d, True).wait_recv()
        proj += inward(ba[h], 0, CA)
        gate, up = proj[:, :FF], proj[:, FF:]
        inner = (gate / (1.0 + jnp.exp(-gate)) * up * weight).astype(BF)
        pa_send[h] = outward(inner, 0, CA)
        for d in ORDER:
            ret_a(h, d, False).start()
        pb_send[h] = outward(dot(perm[h], inner).astype(BF), WA, CB)
        for d in ORDER:
            ret_b(h, d, False).start()
        pa[h, y] = pa_send[h, y]
        pb[h, z] = pb_send[h, z]
        xz, xy, gz = spread_hits(h, t)
        ra[h] = (dot_t(xz, gz) * ma[...]).astype(BF)
        rb[h] = (dot_t(xy, gt[...]) * mb[...]).astype(BF)

        @pl.when(mine == h)
        def _():
            for d in ORDER:
                small_a(h, d, False).wait_send()
                small_b(h, d, False).wait_send()

    def gather(h, t):
        @pl.when(t > 0)
        def _():
            each_home(h, lambda d: (home_a(h, d, False).wait_send(), home_b(h, d, False).wait_send()))
        for d in ORDER:
            ret_b(h, d, True).wait_recv()
        qb_send[h] = dot(rb[h], pb[h].reshape(N * BLK, CB)).astype(BF).reshape(G, 16, CB)
        each_home(h, lambda d: home_b(h, d, False).start())
        for d in ORDER:
            ret_a(h, d, True).wait_recv()
        total = pa[h, 0].astype(F32)
        for i in range(1, N):
            total += pa[h, i].astype(F32)
        qa_send[h] = dot(ra[h], total.astype(BF)).astype(BF).reshape(G, 16, CA)
        each_home(h, lambda d: home_a(h, d, False).start())
        for d in ORDER:
            big_a(h, d, False).wait_send()
            big_b(h, d, False).wait_send()
            ret_a(h, d, False).wait_send()
            ret_b(h, d, False).wait_send()

    def finish(h, t):
        @pl.when(mine == h)
        def _():
            qa[z] = qa_send[h, z // NB]
            qb[y] = qb_send[h, y // NB]
            x = out[t].astype(F32)
            for d in ORDER:
                home_b(h, d, True).wait_recv()
            total_b = qb[0].astype(F32)
            for i in range(1, N):
                total_b += qb[i].astype(F32)
            for d in ORDER:
                home_a(h, d, True).wait_recv()
            total_a = qa[0].astype(F32)
            for i in range(1, N):
                total_a += qa[i].astype(F32)
            out[t, :, :CA] = (x[:, :CA] + total_a).astype(BF)
            out[t, :, CA:] = (x[:, CA:] + total_b).astype(BF)

            @pl.when(jnp.logical_and(s < N - 1, t < N - 1))
            def _():
                hop_copy(t).start()

    for d in ORDER:
        for c in table_copies(d, False):
            c.start()
    hz[at(z)] = hown[...]
    hy[at(y)] = hown[...]

    order = ((begin, 0, 0), (gather, 1, 1), (select, 0, 0), (finish, 1, 1), (begin, 1, 0),
             (experts, 0, 0), (select, 1, 0), (gather, 0, 0), (experts, 1, 0), (finish, 0, 0))

    def tick(t, carry):
        for step, h, late in order:
            @pl.when(t > 0 if late else t < N)
            def _():
                step(h, t - late)
        return carry

    lax.fori_loop(0, N + 1, tick, 0)

    for h in range(NB):
        each_home(h, lambda d: (home_a(h, d, False).wait_send(), home_b(h, d, False).wait_send()))
    for d in ORDER:
        for c in table_copies(d, False):
            c.wait_send()
        weight_copy(d, False).wait_send()

    @pl.when(s < N - 1)
    def _():
        for t in range(N - 1):
            hop_copy(t).wait_send()


def unfolded(blocks):
    lead = blocks.shape[:-2]
    axes = tuple(range(len(lead))) + (len(lead) + 1, len(lead), len(lead) + 2)
    split = blocks.reshape(lead + (4, ROWS, CA + CB)).transpose(axes)
    return jnp.concatenate([split[..., :CA].reshape(lead + (ROWS, WA)),
                            split[..., CA:].reshape(lead + (ROWS, D - WA))], axis=-1)


def constants():
    e1 = np.zeros((G, 4, ROWS, G, 8), np.float32)
    for i in range(G):
        for r in range(ROWS):
            e1[i, :, r, i, r] = 1
    gt = np.zeros((N, 4, G, CAP, 128), np.float32)
    for k in range(N):
        for c in range(CAP):
            gt[k, :, :, c, k * CAP + c] = 1
    mt = np.zeros((4, G, CAP, G, 4, ROWS), np.float32)
    for q in range(4):
        for i in range(G):
            mt[q, i, :, i, q, :] = 1
    mt = mt.reshape(BLK, GR)
    sw = np.zeros((G, CAP, G, 8), np.float32)
    for i in range(G):
        sw[i, :, i, :ROWS] = 1
    perm = np.zeros((NB, N * SL, N * SL), np.float32)
    for k in range(N):
        for j in range(N):
            for c in range(CAP):
                perm[(k + j) % NB, j * SL + k // NB * CAP + c, k * SL + j // NB * CAP + c] = 1
    return (jnp.asarray(e1.reshape(GR, G * 8), BF), jnp.asarray(gt.reshape(N * BLK, 128), BF),
            jnp.asarray(mt), jnp.asarray(mt.T), jnp.asarray(np.tile(mt.T, (1, N))),
            jnp.asarray(perm, BF), jnp.asarray(sw.reshape(SL, G * 8)))


def body(micro_inputs, norm_gain, gate_up, down_proj, routes, route_weights):
    def spread(table, empty):
        wide = jnp.repeat(table.transpose(2, 1, 0), 16, axis=2)
        return jnp.concatenate([wide, jnp.full_like(wide, empty)], axis=1)

    vmem = pl.BlockSpec(memory_space=pltpu.VMEM)
    hbm = pl.BlockSpec(memory_space=pl.ANY)
    out = pl.pallas_call(
        kernel,
        out_shape=jax.ShapeDtypeStruct((N, 16, CA + CB), BF),
        in_specs=[vmem] * 4 + [hbm] * 2 + [vmem] * 7,
        out_specs=vmem,
        scratch_shapes=[
            pltpu.VMEM((16, CA + CB), F32), pltpu.VMEM((8, 128), F32),
            pltpu.VMEM((D, 2 * FF), BF), pltpu.VMEM((FF, D), BF),
            pltpu.VMEM((N, 16, CA + CB), BF),
            pltpu.VMEM((N, 8, 128), F32), pltpu.VMEM((N, 8, 128), F32),
            pltpu.VMEM((N, 64, 128), BF), pltpu.VMEM((N, 64, 128), BF),
            pltpu.VMEM((16, 128), F32), pltpu.VMEM((N, 16, 128), F32),
            pltpu.VMEM((NB, BLK, GR), BF), pltpu.VMEM((NB, N * BLK, GR), BF),
            pltpu.VMEM((NB, GR, BLK), BF), pltpu.VMEM((NB, GR, N * BLK), BF),
            pltpu.VMEM((16, CA), BF), pltpu.VMEM((16, CB), BF),
            pltpu.VMEM((NB, G, 16, CA), BF), pltpu.VMEM((NB, G, 16, CB), BF),
            pltpu.VMEM((NB, BLK, CA), BF), pltpu.VMEM((NB, N, BLK, CB), BF),
            pltpu.VMEM((NB, N, BLK, CA), BF), pltpu.VMEM((NB, N, BLK, CB), BF),
            pltpu.VMEM((NB, N, BLK, CA), BF), pltpu.VMEM((NB, N, BLK, CB), BF),
            pltpu.VMEM((NB, N, BLK, CA), BF), pltpu.VMEM((NB, N, BLK, CB), BF),
            pltpu.VMEM((NB, G, 16, CA), BF), pltpu.VMEM((NB, G, 16, CB), BF),
            pltpu.VMEM((N, 16, CA), BF), pltpu.VMEM((N, 16, CB), BF),
            pltpu.SemaphoreType.DMA((8, NB, N)), pltpu.SemaphoreType.DMA((8, NB, N)),
            pltpu.SemaphoreType.DMA((3, N)), pltpu.SemaphoreType.DMA((3, N)),
            pltpu.SemaphoreType.DMA((N,)), pltpu.SemaphoreType.DMA((N,)),
            pltpu.SemaphoreType.DMA((2,)),
        ],
        compiler_params=pltpu.CompilerParams(
            collective_id=0, has_side_effects=True, vmem_limit_bytes=56 << 20),
    )(micro_inputs, norm_gain, spread(routes[0], -1), spread(route_weights[0], 0.0),
      gate_up, down_proj, *constants())
    return unfolded(out)[None]


def solution(mesh):
    return jax.shard_map(
        body,
        mesh=mesh,
        in_specs=(
            P(None, "expert", None),
            P("section", None),
            P("section", "expert", None, None),
            P("section", "expert", None, None),
            P("section", None, "expert", None),
            P("section", None, "expert", None),
        ),
        out_specs=P("section", None, "expert", None),
        check_vma=False,
    )
```

```python
import numpy as np
import jax
import jax.numpy as jnp
from jax import lax
from jax.experimental import pallas as pl
from jax.experimental.pallas import tpu as pltpu
from jax.sharding import PartitionSpec as P

D = 3584
FF = 128
N = 8
ROWS = 4
CAP = 2
CA = 512
CB = 384
WA = 4 * CA
NB = 4
G = N // NB
SL = G * CAP
GR = G * 16
BLK = 4 * SL
EPSILON = 1e-06
MESH = pl.DeviceIdType.MESH
ORDER = (4, 3, 5, 2, 6, 1, 7)
BF = jnp.bfloat16
F32 = jnp.float32


def dot(a, b):
    return jnp.dot(a, b, preferred_element_type=F32)


def dot_t(a, b):
    return lax.dot_general(a, b, (((1,), (1,)), ((), ())), preferred_element_type=F32)


def exact(a, b):
    return jnp.dot(a, b, preferred_element_type=F32, precision=lax.Precision.HIGHEST)


def folded(x):
    part_a = jnp.concatenate([x[:, q * CA:(q + 1) * CA] for q in range(4)], axis=0)
    part_b = jnp.concatenate([x[:, WA + q * CB:WA + (q + 1) * CB] for q in range(4)], axis=0)
    return jnp.concatenate([part_a, part_b], axis=1)


def kernel(micro, norm_gain, picked, weights, wg_hbm, wd_hbm, e1, gt, mt, ma, mb, perm, sw, out,
           gain, hown, wg, wd, hop, hz, hy, hzt, hyt, wsend, wbuf, la, lb, ra, rb,
           na, nb, sa, sb, ba_send, bb_send, ba, bb, pa_send, pb_send, pa, pb,
           qa_send, qb_send, qa, qb, ssem, rsem, s1, r1, hs, hr, wsem):
    s = lax.axis_index("section")
    e = lax.axis_index("expert")
    z, y = e // N, e % N
    mine = (z + y) % NB

    def on_z(d):
        return (s, ((z + d) % N) * N + y)

    def on_y(d):
        return (s, z * N + (y + d) % N)

    load_g = pltpu.make_async_copy(wg_hbm.at[0, 0], wg, wsem.at[0])
    load_d = pltpu.make_async_copy(wd_hbm.at[0, 0], wd, wsem.at[1])
    load_g.start()
    load_d.start()

    gain[...] = folded(jnp.broadcast_to(norm_gain[...].astype(F32), (ROWS, D)))
    lanes = lax.broadcasted_iota(jnp.int32, (8, 128), 1)
    row = lax.broadcasted_iota(jnp.int32, (8, 128), 0)
    expert = (lanes >> 1) & 7
    first_pick, second_pick = picked[0] == expert, picked[1] == expert
    taken = jnp.where(first_pick | second_pick, 1.0, 0.0)
    ahead = jnp.zeros((8, 128), F32)
    for i in range(1, ROWS):
        ahead += jnp.where(row >= i, pltpu.roll(taken, i, 0), 0.0)
    in_place = (ahead == (lanes & 1).astype(F32)) & (taken > 0)
    hown[...] = jnp.where(in_place, jnp.where(first_pick, weights[0], weights[1]), 0.0)

    bar = pltpu.get_barrier_semaphore()
    for d in range(1, N):
        pl.semaphore_signal(bar, inc=1, device_id=on_z(d), device_id_type=MESH)
        pl.semaphore_signal(bar, inc=1, device_id=on_y(d), device_id_type=MESH)
    pl.semaphore_signal(bar, inc=1, device_id=((s + 1) % N, e), device_id_type=MESH)
    pl.semaphore_signal(bar, inc=1, device_id=((s + N - 1) % N, e), device_id_type=MESH)
    pl.semaphore_wait(bar, 2 * (N - 1) + 2)

    def remote(phase, h, d, src, dst, target):
        return pltpu.make_async_remote_copy(
            src_ref=src, dst_ref=dst, send_sem=ssem.at[phase, h], recv_sem=rsem.at[phase, h],
            device_id=target, device_id_type=MESH)

    def once(phase, d, src, dst, target):
        return pltpu.make_async_remote_copy(
            src_ref=src, dst_ref=dst, send_sem=s1.at[phase, d], recv_sem=r1.at[phase, d],
            device_id=target, device_id_type=MESH)

    def at(v):
        return (v % NB) * G + v // NB

    def table_copies(d, back):
        zz, yy = ((z + N - d) % N, (y + N - d) % N) if back else (z, y)
        return (once(0, d, hown, hz.at[at(zz)], on_z(d)), once(1, d, hown, hy.at[at(yy)], on_y(d)))

    def weight_copy(d, back):
        return once(2, d, wsend, wbuf.at[(y + N - d) % N if back else y], on_y(d))

    def small_a(h, d):
        return remote(0, h, d, na, sa.at[h, z // NB], on_z(d))

    def small_b(h, d):
        return remote(1, h, d, nb, sb.at[h, y // NB], on_y(d))

    def big_a(h, d):
        return remote(2, h, d, ba_send.at[h], ba.at[h, y], on_y(d))

    def big_b(h, d):
        return remote(3, h, d, bb_send.at[h, (z + d) % N], bb.at[h, z],
                      on_z(d))

    def ret_a(h, d):
        return remote(4, h, d, pa_send.at[h, (y + d) % N], pa.at[h, y],
                      on_y(d))

    def ret_b(h, d):
        return remote(5, h, d, pb_send.at[h, (z + d) % N], pb.at[h, z],
                      on_z(d))

    def home_a(h, d):
        return remote(6, h, d, qa_send.at[h, ((z + d) % N) // NB],
                      qa.at[z], on_z(d))

    def home_b(h, d):
        return remote(7, h, d, qb_send.at[h, ((y + d) % N) // NB],
                      qb.at[y], on_y(d))

    def hop_copy(t):
        return pltpu.make_async_remote_copy(
            src_ref=out.at[t], dst_ref=hop.at[t + 1], send_sem=hs.at[t], recv_sem=hr.at[t],
            device_id=((s + 1) % N, e), device_id_type=MESH)

    def all_of(phase, h, size):
        return remote(phase, h, 1, size, size, on_y(1))

    def many_sources(phase, h, buf):
        @pl.when(mine == h)
        def _():
            all_of(phase, h, buf.at[:G - 1]).wait_recv()

        @pl.when(mine != h)
        def _():
            all_of(phase, h, buf).wait_recv()

    def many_homes(phase, h, buf):
        @pl.when(mine == h)
        def _():
            all_of(phase, h, buf.at[:G - 1]).wait_send()

        @pl.when(mine != h)
        def _():
            all_of(phase, h, buf).wait_send()

    def each_home(h, act):
        first = (h + NB - mine) % NB
        for k in range(G - 1, 0, -1):
            act(k * NB + first)

        @pl.when(first != 0)
        def _():
            act(first)

    def spread_hits(h, t):
        from_z = pl.multiple_of(((h + N - y) % NB) * (G * 8), G * 8)
        from_y = pl.multiple_of(((h + N - z) % NB) * (G * 8), G * 8)
        xz = dot(e1[...], hzt[t, pl.ds(from_z, G * 8), :]).astype(BF)
        xy = dot(e1[...], hyt[t, pl.ds(from_y, G * 8), :]).astype(BF)
        return xz, xy, gt[pl.ds(pl.multiple_of(z * BLK, BLK), BLK), :]

    def begin(h, t):
        @pl.when(mine == h)
        def _():
            @pl.when(jnp.logical_or(s == 0, t == 0))
            def _():
                out[t] = folded(micro[t + (s + N - 1) // N * (s + N - 1)].astype(F32)).astype(BF)

            @pl.when(jnp.logical_and(s > 0, t > 0))
            def _():
                hop_copy(t - 1).wait_recv()
                out[t] = hop[t]

            x = out[t].astype(F32)
            ss = jnp.sum(x * x, axis=1, keepdims=True)
            ss = ss + pltpu.roll(ss, 8, 0)
            ss = ss + pltpu.roll(ss, 4, 0)
            n = ((x * lax.rsqrt(ss * (1.0 / D) + EPSILON)) * gain[...]).astype(BF)
            na[...] = n[:, :CA]
            nb[...] = n[:, CA:]
            for d in ORDER:
                small_a(h, d).start()
                small_b(h, d).start()
            sa[h, z // NB] = n[:, :CA]
            sb[h, y // NB] = n[:, CA:]

        if h == 0:
            @pl.when(t == 0)
            def _():
                for d in ORDER:
                    for c in table_copies(d, True):
                        c.wait_recv()
                all_z = hz[...].reshape(64, 128)
                all_y = hy[...].reshape(64, 128)
                for i in range(N):
                    hzt[i] = jnp.where(pltpu.roll(all_z, (128 - 16 * i) % 128, 1) > 0, 1.0, 0.0).astype(BF)
                    hyt[i] = jnp.where(pltpu.roll(all_y, (128 - 16 * i) % 128, 1) > 0, 1.0, 0.0).astype(BF)
                lane = lax.broadcasted_iota(jnp.int32, (128, 128), 0)
                tick_of = lax.broadcasted_iota(jnp.int32, (128, 128), 1)
                pick = jnp.where((lane // 16 == tick_of) & ((lane // 2) % N == z), 1.0, 0.0)
                odd = lax.broadcasted_iota(jnp.int32, (SL, 128), 1) % 2
                row = lax.broadcasted_iota(jnp.int32, (SL, 128), 0) % 2
                for g in range(NB):
                    sums = exact(sw[...], hz[pl.ds(((g + N - y) % NB) * G, G)].reshape(G * 8, 128))
                    wsend[g * SL:(g + 1) * SL, :] = exact(jnp.where(odd == row, sums, 0.0), pick)
                for d in ORDER:
                    weight_copy(d, False).start()
                wbuf[y] = wsend[...]

        xz, xy, gz = spread_hits(h, t)
        la[h] = (dot_t(gz, xz) * mt[...]).astype(BF)
        lb[h] = (dot_t(gt[...], xy).reshape(N, BLK, GR) * mt[...][None]).reshape(N * BLK, GR).astype(BF)

    def select(h, t):
        many_sources(0, h, sa.at[h])
        ba_send[h] = dot(la[h], sa[h].reshape(GR, CA)).astype(BF)
        for d in ORDER:
            big_a(h, d).start()
        ba[h, y] = ba_send[h]
        many_sources(1, h, sb.at[h])
        bb_send[h] = dot(lb[h], sb[h].reshape(GR, CB)).astype(BF).reshape(N, BLK, CB)
        for d in ORDER:
            big_b(h, d).start()
        bb[h, z] = bb_send[h, z]

    def inward(block, first, columns):
        per = 16 // SL
        total = jnp.zeros((N * SL, 2 * FF), F32)
        for q in range(4):
            rows = block[:, q // per * 16:q // per * 16 + 16, :].reshape(N * 16, columns)
            product = dot(rows, wg[first + q * columns:first + (q + 1) * columns, :])
            total += product.reshape(N, per, SL, 2 * FF)[:, q % per].reshape(N * SL, 2 * FF)
        return total

    def outward(rows, first, columns):
        parts = [dot(rows, wd[:, first + q * columns:first + (q + 1) * columns]).reshape(N, SL, columns)
                 for q in range(4)]
        return jnp.concatenate(parts, axis=1).astype(BF)

    def experts(h, t):
        if h == 0:
            @pl.when(t == 0)
            def _():
                load_g.wait()
                load_d.wait()
                for d in ORDER:
                    weight_copy(d, True).wait_recv()
        all_of(3, h, bb.at[h, :N - 1]).wait_recv()
        proj_b = inward(bb[h], WA, CB)
        high = proj_b.astype(BF)
        low = (proj_b - high.astype(F32)).astype(BF)
        proj = dot(perm[h], high) + dot(perm[h], low)
        tick_lane = lax.broadcasted_iota(jnp.int32, (N * SL, 128), 1) == t
        weight = jnp.sum(jnp.where(tick_lane, wbuf[:, SL * h:SL * h + SL, :].reshape(N * SL, 128), 0.0),
                         axis=1, keepdims=True)
        all_of(2, h, ba.at[h, :N - 1]).wait_recv()
        proj += inward(ba[h], 0, CA)
        gate, up = proj[:, :FF], proj[:, FF:]
        inner = (gate / (1.0 + jnp.exp(-gate)) * up * weight).astype(BF)
        pa_send[h] = outward(inner, 0, CA)
        for d in ORDER:
            ret_a(h, d).start()
        pb_send[h] = outward(dot(perm[h], inner).astype(BF), WA, CB)
        for d in ORDER:
            ret_b(h, d).start()
        pa[h, y] = pa_send[h, y]
        pb[h, z] = pb_send[h, z]
        xz, xy, gz = spread_hits(h, t)
        ra[h] = (dot_t(xz, gz) * ma[...]).astype(BF)
        rb[h] = (dot_t(xy, gt[...]) * mb[...]).astype(BF)

        @pl.when(mine == h)
        def _():
            all_of(0, h, qa.at[:N - 1]).wait_send()
            all_of(1, h, qb.at[:N - 1]).wait_send()

    def gather(h, t):
        @pl.when(t > 0)
        def _():
            many_homes(6, h, qa_send.at[h])
            many_homes(7, h, qb_send.at[h])

        all_of(5, h, pb.at[h, :N - 1]).wait_recv()
        qb_send[h] = dot(rb[h], pb[h].reshape(N * BLK, CB)).astype(BF).reshape(G, 16, CB)
        each_home(h, lambda d: home_b(h, d).start())
        all_of(4, h, pa.at[h, :N - 1]).wait_recv()
        total = pa[h, 0].astype(F32)
        for i in range(1, N):
            total += pa[h, i].astype(F32)
        qa_send[h] = dot(ra[h], total.astype(BF)).astype(BF).reshape(G, 16, CA)
        each_home(h, lambda d: home_a(h, d).start())
        for phase, buf in ((2, ba), (3, bb), (4, pa), (5, pb)):
            all_of(phase, h, buf.at[h, :N - 1]).wait_send()

    def finish(h, t):
        @pl.when(mine == h)
        def _():
            qa[z] = qa_send[h, z // NB]
            qb[y] = qb_send[h, y // NB]
            x = out[t].astype(F32)
            all_of(7, h, qb.at[:N - 1]).wait_recv()
            total_b = qb[0].astype(F32)
            for i in range(1, N):
                total_b += qb[i].astype(F32)
            all_of(6, h, qa.at[:N - 1]).wait_recv()
            total_a = qa[0].astype(F32)
            for i in range(1, N):
                total_a += qa[i].astype(F32)
            out[t, :, :CA] = (x[:, :CA] + total_a).astype(BF)
            out[t, :, CA:] = (x[:, CA:] + total_b).astype(BF)

            @pl.when(jnp.logical_and(s < N - 1, t < N - 1))
            def _():
                hop_copy(t).start()

    for d in ORDER:
        for c in table_copies(d, False):
            c.start()
    hz[at(z)] = hown[...]
    hy[at(y)] = hown[...]

    order = ((begin, 0, 0), (begin, 1, 0), (gather, 2, 1), (gather, 3, 1), (select, 0, 0),
             (select, 1, 0), (finish, 2, 1), (finish, 3, 1), (begin, 2, 0), (begin, 3, 0),
             (experts, 0, 0), (experts, 1, 0), (select, 2, 0), (select, 3, 0), (gather, 0, 0),
             (gather, 1, 0), (experts, 2, 0), (experts, 3, 0), (finish, 0, 0), (finish, 1, 0))

    def tick(t, carry):
        for step, h, late in order:
            @pl.when(t > 0 if late else t < N)
            def _():
                step(h, t - late)
        return carry

    lax.fori_loop(0, N + 1, tick, 0)

    for h in range(NB):
        many_homes(6, h, qa_send.at[h])
        many_homes(7, h, qb_send.at[h])
    for d in ORDER:
        for c in table_copies(d, False):
            c.wait_send()
        weight_copy(d, False).wait_send()

    @pl.when(s < N - 1)
    def _():
        for t in range(N - 1):
            hop_copy(t).wait_send()


def unfolded(blocks):
    lead = blocks.shape[:-2]
    axes = tuple(range(len(lead))) + (len(lead) + 1, len(lead), len(lead) + 2)
    split = blocks.reshape(lead + (4, ROWS, CA + CB)).transpose(axes)
    return jnp.concatenate([split[..., :CA].reshape(lead + (ROWS, WA)),
                            split[..., CA:].reshape(lead + (ROWS, D - WA))], axis=-1)


def constants():
    e1 = np.zeros((G, 4, ROWS, G, 8), np.float32)
    for i in range(G):
        for r in range(ROWS):
            e1[i, :, r, i, r] = 1
    gt = np.zeros((N, 4, G, CAP, 128), np.float32)
    for k in range(N):
        for c in range(CAP):
            gt[k, :, :, c, k * CAP + c] = 1
    mt = np.zeros((4, G, CAP, G, 4, ROWS), np.float32)
    for q in range(4):
        for i in range(G):
            mt[q, i, :, i, q, :] = 1
    mt = mt.reshape(BLK, GR)
    sw = np.zeros((G, CAP, G, 8), np.float32)
    for i in range(G):
        sw[i, :, i, :ROWS] = 1
    perm = np.zeros((NB, N * SL, N * SL), np.float32)
    for k in range(N):
        for j in range(N):
            for c in range(CAP):
                perm[(k + j) % NB, j * SL + k // NB * CAP + c, k * SL + j // NB * CAP + c] = 1
    return (jnp.asarray(e1.reshape(GR, G * 8), BF), jnp.asarray(gt.reshape(N * BLK, 128), BF),
            jnp.asarray(mt), jnp.asarray(mt.T), jnp.asarray(np.tile(mt.T, (1, N))),
            jnp.asarray(perm, BF), jnp.asarray(sw.reshape(SL, G * 8)))


def body(micro_inputs, norm_gain, gate_up, down_proj, routes, route_weights):
    def spread(table, empty):
        wide = jnp.repeat(table.transpose(2, 1, 0), 16, axis=2)
        return jnp.concatenate([wide, jnp.full_like(wide, empty)], axis=1)

    vmem = pl.BlockSpec(memory_space=pltpu.VMEM)
    hbm = pl.BlockSpec(memory_space=pl.ANY)
    out = pl.pallas_call(
        kernel,
        out_shape=jax.ShapeDtypeStruct((N, 16, CA + CB), BF),
        in_specs=[vmem] * 4 + [hbm] * 2 + [vmem] * 7,
        out_specs=vmem,
        scratch_shapes=[
            pltpu.VMEM((16, CA + CB), F32), pltpu.VMEM((8, 128), F32),
            pltpu.VMEM((D, 2 * FF), BF), pltpu.VMEM((FF, D), BF),
            pltpu.VMEM((N, 16, CA + CB), BF),
            pltpu.VMEM((N, 8, 128), F32), pltpu.VMEM((N, 8, 128), F32),
            pltpu.VMEM((N, 64, 128), BF), pltpu.VMEM((N, 64, 128), BF),
            pltpu.VMEM((16, 128), F32), pltpu.VMEM((N, 16, 128), F32),
            pltpu.VMEM((NB, BLK, GR), BF), pltpu.VMEM((NB, N * BLK, GR), BF),
            pltpu.VMEM((NB, GR, BLK), BF), pltpu.VMEM((NB, GR, N * BLK), BF),
            pltpu.VMEM((16, CA), BF), pltpu.VMEM((16, CB), BF),
            pltpu.VMEM((NB, G, 16, CA), BF), pltpu.VMEM((NB, G, 16, CB), BF),
            pltpu.VMEM((NB, BLK, CA), BF), pltpu.VMEM((NB, N, BLK, CB), BF),
            pltpu.VMEM((NB, N, BLK, CA), BF), pltpu.VMEM((NB, N, BLK, CB), BF),
            pltpu.VMEM((NB, N, BLK, CA), BF), pltpu.VMEM((NB, N, BLK, CB), BF),
            pltpu.VMEM((NB, N, BLK, CA), BF), pltpu.VMEM((NB, N, BLK, CB), BF),
            pltpu.VMEM((NB, G, 16, CA), BF), pltpu.VMEM((NB, G, 16, CB), BF),
            pltpu.VMEM((N, 16, CA), BF), pltpu.VMEM((N, 16, CB), BF),
            pltpu.SemaphoreType.DMA((8, NB)), pltpu.SemaphoreType.DMA((8, NB)),
            pltpu.SemaphoreType.DMA((3, N)), pltpu.SemaphoreType.DMA((3, N)),
            pltpu.SemaphoreType.DMA((N,)), pltpu.SemaphoreType.DMA((N,)),
            pltpu.SemaphoreType.DMA((2,)),
        ],
        compiler_params=pltpu.CompilerParams(
            collective_id=0, has_side_effects=True, vmem_limit_bytes=56 << 20),
    )(micro_inputs, norm_gain, spread(routes[0], -1), spread(route_weights[0], 0.0),
      gate_up, down_proj, *constants())
    return unfolded(out)[None]


def solution(mesh):
    return jax.shard_map(
        body,
        mesh=mesh,
        in_specs=(
            P(None, "expert", None),
            P("section", None),
            P("section", "expert", None, None),
            P("section", "expert", None, None),
            P("section", None, "expert", None),
            P("section", None, "expert", None),
        ),
        out_specs=P("section", None, "expert", None),
        check_vma=False,
    )
```
